512 devices in a mesh: gx: 32 (over y, x), gy: 4 (over z_lo), gz: 4 (over z_hi, core).
Axes of the slice: x: 4, y: 8, z: 8 (z_hi: 2, z_lo: 4; z = z_hi * 4 + z_lo), core: 2. Of those that a mesh axis runs over, the one named last changes fastest.
Arguments:
- volume: float32 [1024, 128, 1024], P('gx', 'gz', 'gy'), may hold values from -18 to 18, as said below
- start_block: float32 [1024, 256], replicated, may hold values from -6 to 6
Outputs:
- factor: float32 [1024, 256], P('gx')
- core_block: float32 [256, 128, 1024], P(('gx', 'gy'), 'gz')
The draws below stay inside these ranges and needn't reach their ends.
Inputs may be any that keep to these rules, and one draw needn't show every extreme that they name: `volume`: finite entries of order one.
All inputs are finite; a program needn't handle non-finite values.
Results may differ from the reference program's by a relative error of at most 0.0003.
Values sent between devices are 32-bit elements; how exact they have to be, the bound alone decides.
No kernel may reach another device: no remote copies, remote signals or barrier semaphores. Data moves between devices by JAX's collectives and lax.ppermute only.
A program may use at most 64 MiB of HBM per device.

```python
import jax
import jax.numpy as jnp
from jax import lax

N1 = 1024
N2 = 1024
RANK = 256
ITERS = 4
N3 = 128


def draw_volume(key, part):
    key = jax.random.fold_in(key, 11)
    keys = jax.random.split(key, 3)
    row_scale = jnp.exp(jax.random.uniform(keys[0], (N1, 1, 1), jnp.float32, jnp.log(0.3), jnp.log(3.0)))
    col_scale = jnp.exp(jax.random.uniform(keys[1], (1, 1, N2), jnp.float32, jnp.log(0.3), jnp.log(3.0)))
    base = jax.random.normal(keys[2], (N1, N3, N2), jnp.float32)
    base = jnp.clip(base, -5.0, 5.0)
    return (0.4 * base * row_scale * col_scale).astype(jnp.float32)


def noise(own_key, dims, spread, bound, held_as=jnp.bfloat16):
    values = spread * jax.random.normal(own_key, dims, jnp.float32)
    return jnp.clip(values, min=-bound, max=bound).astype(held_as)


def setup_inputs(seed: int = 0) -> dict:
    seeds = jax.random.split(jax.random.key(seed), 3)
    volume = draw_volume(jax.random.fold_in(seeds[2], 71), 0)
    start_block = noise(seeds[1], (N1, RANK), 1.0, 6.0, jnp.float32)
    return {"volume": volume, "start_block": start_block}


def orthonormal(applied):
    highest = lax.Precision.HIGHEST
    products = jnp.dot(applied.T.astype(jnp.float32), applied.astype(jnp.float32), precision=highest, preferred_element_type=jnp.float32)
    factor_low = jnp.linalg.cholesky(products)
    return lax.linalg.triangular_solve(factor_low, applied, left_side=False, lower=True, transpose_a=True)

def reference(volume, start_block):
    highest = lax.Precision.HIGHEST
    flattened = volume.reshape(N1, N3 * N2)
    gram = jnp.dot(flattened.astype(jnp.float32), flattened.T.astype(jnp.float32), precision=highest, preferred_element_type=jnp.float32) * (1.0 / (N2 * N3))
    subspace = start_block
    for iteration in range(ITERS):
        applied = jnp.dot(gram.astype(jnp.float32), subspace.astype(jnp.float32), precision=highest, preferred_element_type=jnp.float32)
        subspace = orthonormal(applied)
    core_block = jnp.einsum('azc,ar->rzc', volume, subspace, precision=highest)
    return (subspace, core_block)
```

```python
import jax
import jax.numpy as jnp
from jax import lax
from jax.experimental import pallas as pl
from jax.experimental.pallas import tpu as pltpu
from jax.sharding import Mesh, PartitionSpec as P

ITERS = 4
TILE = 128
HIGHEST = lax.Precision.HIGHEST


def triangle(tiles):
    return [(i, j) for i in range(tiles) for j in range(i + 1)]


def gram_kernel(fibres_ref, packed_ref):
    tiles = fibres_ref.shape[0] // TILE
    for pair in range(tiles // 2):
        rows = fibres_ref[pl.ds(2 * TILE * pair, 2 * TILE), :]
        block = lax.dot_general(
            rows,
            fibres_ref[pl.ds(0, 2 * TILE * (pair + 1)), :],
            (((1,), (1,)), ((), ())),
            precision=HIGHEST,
            preferred_element_type=jnp.float32,
        )
        for half in range(2):
            i = 2 * pair + half
            for j in range(i + 1):
                place = (i * (i + 1)) // 2 + j
                packed_ref[pl.ds(place * TILE, TILE), :] = block[
                    half * TILE : (half + 1) * TILE, j * TILE : (j + 1) * TILE
                ]


def packed_gram(fibres):
    rows = fibres.shape[0]
    count = len(triangle(rows // TILE))
    return pl.pallas_call(
        gram_kernel,
        out_shape=jax.ShapeDtypeStruct((count * TILE, TILE), jnp.float32),
        compiler_params=pltpu.CompilerParams(vmem_limit_bytes=32 * 1024 * 1024),
    )(fibres)


def unpack_kernel(scaling, packed_ref, gram_ref):
    tiles = gram_ref.shape[0] // TILE
    for place, (i, j) in enumerate(triangle(tiles)):
        block = packed_ref[pl.ds(place * TILE, TILE), :] * scaling
        gram_ref[pl.ds(i * TILE, TILE), pl.ds(j * TILE, TILE)] = block
        if i != j:
            gram_ref[pl.ds(j * TILE, TILE), pl.ds(i * TILE, TILE)] = block.T


def unpacked_gram(packed, rows, scaling):
    def kernel(packed_ref, gram_ref):
        unpack_kernel(scaling, packed_ref, gram_ref)

    return pl.pallas_call(
        kernel,
        out_shape=jax.ShapeDtypeStruct((rows, rows), jnp.float32),
        compiler_params=pltpu.CompilerParams(vmem_limit_bytes=32 * 1024 * 1024),
    )(packed)


def reduce_scatter(values, axis):
    size = lax.axis_size(axis)
    shares = lax.all_to_all(values, axis, split_axis=0, concat_axis=0, tiled=True)
    return jnp.sum(shares.reshape(size, -1, TILE), axis=0)


def gather(share, axis):
    size = lax.axis_size(axis)
    copies = jnp.broadcast_to(share[None], (size,) + share.shape)
    copies = lax.all_to_all(copies, axis, split_axis=0, concat_axis=0, tiled=True)
    return copies


def sum_over_devices(packed):
    share = packed
    for axis in ("c", "x", "y"):
        share = reduce_scatter(share, axis)
    share = jnp.sum(gather(share, ("zl", "zh")), axis=0)
    for axis in ("y", "x", "c"):
        share = gather(share, axis).reshape(-1, TILE)
    return share


def orthonormal(applied):
    products = jnp.dot(applied.T, applied, precision=HIGHEST, preferred_element_type=jnp.float32)
    factor_low = jnp.linalg.cholesky(products)
    return lax.linalg.triangular_solve(
        factor_low, applied, left_side=False, lower=True, transpose_a=True
    )


def shards(volume, start_block):
    rows_dev, planes, cols_dev = volume.shape
    xy = ("y", "x")
    flattened = volume.reshape(rows_dev, planes * cols_dev)
    fibres = lax.all_to_all(flattened, xy, split_axis=1, concat_axis=0, tiled=True)
    rows = fibres.shape[0]
    scaling = 1.0 / (fibres.shape[1] * lax.axis_size(("y", "x", "zl", "zh", "c")))
    packed = sum_over_devices(packed_gram(fibres))
    gram = unpacked_gram(packed, rows, scaling)
    subspace = start_block
    for iteration in range(ITERS):
        applied = jnp.dot(gram, subspace, precision=HIGHEST, preferred_element_type=jnp.float32)
        subspace = orthonormal(applied)
    row_offset = lax.axis_index(xy) * rows_dev
    own_rows = lax.dynamic_slice_in_dim(subspace, row_offset, rows_dev, 0)
    core_columns = jnp.dot(
        subspace.T, fibres, precision=HIGHEST, preferred_element_type=jnp.float32
    )
    peers = lax.axis_size(("y", "x", "zl"))
    shares = core_columns.reshape(peers, -1, cols_dev)
    shares = lax.all_to_all(shares, ("y", "x", "zl"), split_axis=0, concat_axis=0, tiled=True)
    shares = shares.reshape(planes, -1, shares.shape[1], cols_dev)
    core_block = shares.transpose(2, 0, 1, 3).reshape(shares.shape[2], planes, -1)
    return (own_rows, core_block)


def solution(mesh):
    fine = Mesh(mesh.devices.reshape(8, 4, 4, 2, 2), ("y", "x", "zl", "zh", "c"))
    return jax.shard_map(
        shards,
        mesh=fine,
        in_specs=(P(("y", "x"), ("zh", "c"), "zl"), P()),
        out_specs=(P(("y", "x"), None), P(("y", "x", "zl"), ("zh", "c"), None)),
        check_vma=False,
    )
```

```python
import jax
import jax.numpy as jnp
from jax import lax
from jax.experimental import pallas as pl
from jax.experimental.pallas import tpu as pltpu
from jax.sharding import Mesh, PartitionSpec as P

ITERS = 4
TILE = 128
SUB = 8
PANEL = 64
HIGHEST = lax.Precision.HIGHEST


def triangle(tiles):
    return [(i, j) for i in range(tiles) for j in range(i + 1)]


def unpack(scaling, packed_ref, gram_ref):
    tiles = gram_ref.shape[0] // TILE
    for place, (i, j) in enumerate(triangle(tiles)):
        block = packed_ref[pl.ds(place * TILE, TILE), :] * scaling
        gram_ref[pl.ds(i * TILE, TILE), pl.ds(j * TILE, TILE)] = block
        if i != j:
            gram_ref[pl.ds(j * TILE, TILE), pl.ds(i * TILE, TILE)] = block.T


def reciprocal(x):
    r = pl.reciprocal(x, approx=True)
    r = r * (2.0 - x * r)
    return r * (2.0 - x * r)


def inverse_root(x):
    y = lax.rsqrt(x)
    return y * (1.5 - 0.5 * x * y * y)


def along_lanes(x, j):
    return jnp.broadcast_to(x[:, j : j + 1], (SUB, TILE))


def along_sublanes(x, i):
    return jnp.broadcast_to(x[i : i + 1, :], (SUB, TILE))


def factor_panel(work, panel, rec_ref):
    sub = lax.broadcasted_iota(jnp.int32, (SUB, TILE), 0)
    lane = lax.broadcasted_iota(jnp.int32, (SUB, TILE), 1)
    first = panel * PANEL // SUB
    tiles = list(range(first, first + PANEL // SUB))
    for k in tiles:
        home, off = (k * SUB) // TILE, (k * SUB) % TILE
        inside = (lane >= off) & (lane < off + SUB)
        cols = {t: [along_lanes(work[t, home], off + j) for j in range(SUB)] for t in tiles if t >= k}
        unit = jnp.where(lane - off == sub, 1.0, 0.0)
        for t in tiles:
            if t == k:
                work[t, home] = jnp.where(inside, unit, work[t, home])
            elif t > k:
                work[t, home] = jnp.where(inside, 0.0, work[t, home])
        rec = jnp.ones((SUB, TILE), jnp.float32)
        for j in range(SUB):
            r = reciprocal(along_sublanes(cols[k][j], j))
            rec = jnp.where(sub == j, r, rec)
            upper = [along_sublanes(cols[k][l], j) if l > j else None for l in range(SUB)]
            row = [along_sublanes(work[k, h], j) for h in range(2)]
            for t in tiles:
                if t < k:
                    continue
                m = cols[t][j] * r
                if t == k:
                    m = jnp.where(sub > j, m, 0.0)
                for l in range(j + 1, SUB):
                    cols[t][l] = cols[t][l] - m * upper[l]
                for h in range(2):
                    work[t, h] = work[t, h] - m * row[h]
        rec_ref[pl.ds(k * SUB, SUB), :] = rec


def inverse_factor(prod_ref, rec_ref):
    order = prod_ref.shape[0]
    halves = order // TILE
    for panel in range(order // PANEL):
        start = panel * PANEL
        work = {}
        for t in range(start // SUB, (start + PANEL) // SUB):
            for h in range(halves):
                work[t, h] = prod_ref[pl.ds(t * SUB, SUB), pl.ds(h * TILE, TILE)]
        factor_panel(work, panel, rec_ref)
        for (t, h), value in work.items():
            prod_ref[pl.ds(t * SUB, SUB), pl.ds(h * TILE, TILE)] = value
        rest = order - start - PANEL
        if rest:
            rows = prod_ref[pl.ds(start, PANEL), :]
            rec = rec_ref[pl.ds(start, PANEL), :]
            low = (start + PANEL) // TILE * TILE
            scaled = jnp.concatenate([rows[:, h * TILE : (h + 1) * TILE] * rec for h in range(low // TILE, halves)], axis=1)
            r_io = lax.broadcasted_iota(jnp.int32, rows.shape, 0) + start
            c_io = lax.broadcasted_iota(jnp.int32, rows.shape, 1)
            lower = jnp.where((c_io > r_io) & (c_io < start + PANEL), 0.0, rows)
            update = lax.dot_general(scaled, lower, (((0,), (0,)), ((), ())), precision=HIGHEST, preferred_element_type=jnp.float32)
            update = update[start + PANEL - low :, :]
            old = prod_ref[pl.ds(start + PANEL, rest), :]
            c_io = lax.broadcasted_iota(jnp.int32, old.shape, 1)
            old = jnp.where((c_io >= start) & (c_io < start + PANEL), 0.0, old)
            prod_ref[pl.ds(start + PANEL, rest), :] = old - update
    root = inverse_root(rec_ref[...])
    root = rec_ref[...] * root
    r_io = lax.broadcasted_iota(jnp.int32, (order, TILE), 0)
    for h in range(halves):
        c_io = lax.broadcasted_iota(jnp.int32, (order, TILE), 1) + h * TILE
        value = prod_ref[:, pl.ds(h * TILE, TILE)]
        prod_ref[:, pl.ds(h * TILE, TILE)] = jnp.where(c_io <= r_io, value * root, 0.0)


def iterate_kernel(scaling, own_ref, packed_ref, start_ref, fibres_ref, rows_ref, core_ref, gram_ref, sub_ref, app_ref, prod_ref, rec_ref):
    unpack(scaling, packed_ref, gram_ref)
    sub_ref[...] = start_ref[...]
    chunk = 256
    chunks = gram_ref.shape[0] // chunk

    @pl.loop(0, ITERS)
    def _(step):
        prod_ref[...] = jnp.zeros_like(prod_ref)

        @pl.loop(0, chunks)
        def _(i):
            part = jnp.dot(gram_ref[pl.ds(i * chunk, chunk), :], sub_ref[...], precision=HIGHEST, preferred_element_type=jnp.float32)
            app_ref[pl.ds(i * chunk, chunk), :] = part
            prod_ref[...] += lax.dot_general(part, part, (((0,), (0,)), ((), ())), precision=HIGHEST, preferred_element_type=jnp.float32)

        inverse_factor(prod_ref, rec_ref)

        @pl.loop(0, chunks)
        def _(i):
            sub_ref[pl.ds(i * chunk, chunk), :] = lax.dot_general(
                app_ref[pl.ds(i * chunk, chunk), :], prod_ref[...], (((1,), (1,)), ((), ())), precision=HIGHEST, preferred_element_type=jnp.float32)

    own = rows_ref.shape[0]
    rows_ref[...] = sub_ref[pl.ds(pl.multiple_of(own_ref[0] * own, own), own), :]
    core_ref[...] = lax.dot_general(sub_ref[...], fibres_ref[...], (((0,), (0,)), ((), ())), precision=HIGHEST, preferred_element_type=jnp.float32)


def iterate(packed, start, fibres, own, own_rows, scaling):
    rows, rank = start.shape
    def kernel(*refs):
        iterate_kernel(scaling, *refs)
    vmem = pl.BlockSpec(memory_space=pltpu.VMEM)
    return pl.pallas_call(
        kernel,
        out_shape=(jax.ShapeDtypeStruct((own_rows, rank), jnp.float32), jax.ShapeDtypeStruct((rank, fibres.shape[1]), jnp.float32)),
        in_specs=[pl.BlockSpec(memory_space=pltpu.SMEM), vmem, vmem, vmem],
        out_specs=(vmem, vmem),
        scratch_shapes=[pltpu.VMEM((rows, rows), jnp.float32), pltpu.VMEM((rows, rank), jnp.float32), pltpu.VMEM((rows, rank), jnp.float32),
                        pltpu.VMEM((rank, rank), jnp.float32), pltpu.VMEM((rank, TILE), jnp.float32)],
        compiler_params=pltpu.CompilerParams(vmem_limit_bytes=48 * 1024 * 1024),
    )(own, packed, start, fibres)


def gram_kernel(fibres_ref, packed_ref):
    tiles = fibres_ref.shape[0] // TILE
    for pair in range(tiles // 2):
        rows = fibres_ref[pl.ds(2 * TILE * pair, 2 * TILE), :]
        block = lax.dot_general(
            rows,
            fibres_ref[pl.ds(0, 2 * TILE * (pair + 1)), :],
            (((1,), (1,)), ((), ())),
            precision=HIGHEST,
            preferred_element_type=jnp.float32,
        )
        for half in range(2):
            i = 2 * pair + half
            for j in range(i + 1):
                place = (i * (i + 1)) // 2 + j
                packed_ref[pl.ds(place * TILE, TILE), :] = block[
                    half * TILE : (half + 1) * TILE, j * TILE : (j + 1) * TILE
                ]


def packed_gram(fibres):
    rows = fibres.shape[0]
    count = len(triangle(rows // TILE))
    return pl.pallas_call(
        gram_kernel,
        out_shape=jax.ShapeDtypeStruct((count * TILE, TILE), jnp.float32),
        compiler_params=pltpu.CompilerParams(vmem_limit_bytes=32 * 1024 * 1024),
    )(fibres)


def reduce_scatter(values, axis):
    size = lax.axis_size(axis)
    shares = lax.all_to_all(values, axis, split_axis=0, concat_axis=0, tiled=True)
    return jnp.sum(shares.reshape(size, -1, TILE), axis=0)


def gather(share, axis):
    size = lax.axis_size(axis)
    copies = jnp.broadcast_to(share[None], (size,) + share.shape)
    copies = lax.all_to_all(copies, axis, split_axis=0, concat_axis=0, tiled=True)
    return copies


def sum_over_devices(packed):
    share = packed
    for axis in ("c", "x", "y"):
        share = reduce_scatter(share, axis)
    share = jnp.sum(gather(share, ("zl", "zh")), axis=0)
    for axis in ("y", "x", "c"):
        share = gather(share, axis).reshape(-1, TILE)
    return share


def shards(volume, start_block):
    rows_dev, planes, cols_dev = volume.shape
    xy = ("y", "x")
    flattened = volume.reshape(rows_dev, planes * cols_dev)
    fibres = lax.all_to_all(flattened, xy, split_axis=1, concat_axis=0, tiled=True)
    scaling = 1.0 / (fibres.shape[1] * lax.axis_size(("y", "x", "zl", "zh", "c")))
    packed = sum_over_devices(packed_gram(fibres))
    own_rows, core_columns = iterate(
        packed, start_block, fibres, lax.axis_index(xy).reshape(1), rows_dev, scaling
    )
    peers = lax.axis_size(("y", "x", "zl"))
    shares = core_columns.reshape(peers, -1, cols_dev)
    shares = lax.all_to_all(shares, ("y", "x", "zl"), split_axis=0, concat_axis=0, tiled=True)
    shares = shares.reshape(planes, -1, shares.shape[1], cols_dev)
    core_block = shares.transpose(2, 0, 1, 3).reshape(shares.shape[2], planes, -1)
    return (own_rows, core_block)


def solution(mesh):
    fine = Mesh(mesh.devices.reshape(8, 4, 4, 2, 2), ("y", "x", "zl", "zh", "c"))
    return jax.shard_map(
        shards,
        mesh=fine,
        in_specs=(P(("y", "x"), ("zh", "c"), "zl"), P()),
        out_specs=(P(("y", "x"), None), P(("y", "x", "zl"), ("zh", "c"), None)),
        check_vma=False,
    )
```
